32 devices in a mesh: group: 8 (over y, x, core), fsdp: 4 (over z).
Axes of the slice: x: 2, y: 2, z: 4, core: 2. Of those that a mesh axis runs over, the one named last changes fastest.
Arguments:
- query_embeddings: bfloat16 [128, 4096], P(('group', 'fsdp')), may hold values from -4 to 4
- passage_embeddings: bfloat16 [128, 4096], P(('group', 'fsdp')), may hold values from -4 to 4
- positives: int32 [128], P(('group', 'fsdp')), may hold values from 0 to 127, each once
- logarithm_scale: float32 [], replicated, may hold values from 2.4 to 2.8
- residual_input: bfloat16 [32, 256, 4096], P(('group', 'fsdp')), may hold values from -6 to 6
- attention_head_outputs: bfloat16 [32, 256, 4096], P(('group', 'fsdp')), may hold values from -6 to 6
- output_weight: bfloat16 [4096, 4096], P('fsdp'), may hold values from -0.09375 to 0.09375
- adapter_down_weight: bfloat16 [4096, 16], replicated, may hold values from -0.09375 to 0.09375
- adapter_up_weight: bfloat16 [16, 4096], replicated, may hold values from -0.375 to 0.375
- final_norm_weight: float32 [4096], replicated, may hold values from 0.5 to 1.5
- lengths: int32 [32], P(('group', 'fsdp')), may hold values from 64 to 256
Outputs:
- loss: float32 [], replicated
- scale_grad: float32 [], replicated
- query_grad: float32 [128, 4096], P(('group', 'fsdp'))
- passage_grad: float32 [128, 4096], P(('group', 'fsdp'))
- attn_grad: bfloat16 [32, 256, 4096], P(('group', 'fsdp'))
- residual_grad: bfloat16 [32, 256, 4096], P(('group', 'fsdp'))
- lora_down_grad: float32 [4096, 16], replicated
- lora_up_grad: float32 [16, 4096], replicated
The draws below stay inside these ranges and needn't reach their ends.
All inputs are finite; a program needn't handle non-finite values.
Results may differ from the reference program's by a relative error of at most 0.01.
Values may be sent and summed in bfloat16 or wider, within the bound.
A program may use at most 128 MiB of HBM per device.

```python
import jax
import jax.numpy as jnp
from jax import lax

MODEL_DIMENSION = 4096
HEAD_FEATURES = 4096
ADAPTER_RANK = 16
SEQ = 256
ROWS_DEV = 1
Q_DEV = 4
B = 128
SEQS = 32


def draw_pair(key):
    base = jax.random.fold_in(key, 17)
    keys = jax.random.split(base, 2)
    queries = 0.06 * jax.random.normal(keys[0], (B, MODEL_DIMENSION), jnp.float32)
    passages = 0.06 * jax.random.normal(keys[1], (B, MODEL_DIMENSION), jnp.float32)
    return (jnp.clip(queries, -4.0, 4.0), jnp.clip(passages, -4.0, 4.0))


def draw_query_embeddings(key, part):
    return draw_pair(key)[0].astype(jnp.bfloat16)


def draw_passage_embeddings(key, part):
    return draw_pair(key)[1].astype(jnp.bfloat16)


def touch_ends(result, stream_key, smallest, high):
    longest = result.shape.index(max(result.shape))
    spots = []
    for shift in (0, 1):
        where = [jax.random.randint(jax.random.fold_in(stream_key, axis), (), 0, length) for axis, length in enumerate(result.shape)]
        where[longest] = (where[longest] + shift) % result.shape[longest]
        spots.append(tuple(where))
    return result.at[spots[0]].set(smallest).at[spots[1]].set(high)


def block_scale(stream_key, extent, shards, smallest, high):
    def one(dim, parts):
        steps = jax.random.uniform(jax.random.fold_in(jax.random.fold_in(stream_key, 6), dim), (parts,), jnp.float32, smallest / len(shards), high / len(shards))
        return jnp.repeat(jnp.exp(steps), extent[dim] // parts).reshape((-1,) + (1,) * (len(extent) - dim - 1))

    gain = one(*shards[0])
    for cut in shards[1:]:
        gain = gain * one(*cut)
    return gain


def noise(key, extent, width, limit, cuts=(), kind=jnp.bfloat16):
    entries = jax.random.normal(key, extent, jnp.float32) * width
    if len(cuts) > 0:
        entries = block_scale(key, extent, cuts, -0.22, 0.18) * entries
    return jnp.clip(entries, min=-limit, max=limit).astype(kind)


def setup_inputs(seed: int = 0) -> dict:
    streams_of = jax.random.split(jax.random.key(seed), 12)
    query_embeddings = draw_query_embeddings(jax.random.fold_in(streams_of[11], 71), 0)
    passage_embeddings = draw_passage_embeddings(jax.random.fold_in(streams_of[11], 71), 0)
    positives = jax.random.permutation(streams_of[2], B).astype(jnp.int32)
    logarithm_scale = jnp.clip(jax.random.uniform(streams_of[3], (), jnp.float32, 2.4, 2.8), 2.4, 2.8)
    residual_input = noise(streams_of[4], (SEQS, SEQ, MODEL_DIMENSION), 1.0, 6.0, ((0, 32),))
    attention_head_outputs = noise(streams_of[5], (SEQS, SEQ, HEAD_FEATURES), 1.0, 6.0, ((0, 32),))
    output_weight = noise(streams_of[6], (HEAD_FEATURES, MODEL_DIMENSION), HEAD_FEATURES ** -0.5, 0.09375, ((0, 4),))
    adapter_down_weight = noise(streams_of[7], (HEAD_FEATURES, ADAPTER_RANK), HEAD_FEATURES ** -0.5, 0.09375)
    adapter_up_weight = noise(streams_of[8], (ADAPTER_RANK, MODEL_DIMENSION), (ADAPTER_RANK * 16) ** -0.5, 0.375)
    final_norm_weight = jnp.clip(1.0 + 0.1 * jax.random.normal(streams_of[9], (MODEL_DIMENSION,), jnp.float32), 0.5, 1.5)
    lengths = touch_ends(jax.random.randint(streams_of[10], (SEQS,), SEQ // 4, SEQ + 1), jax.random.fold_in(streams_of[10], 1), SEQ // 4, SEQ).astype(jnp.int32)
    return dict(query_embeddings=query_embeddings, passage_embeddings=passage_embeddings, positives=positives, logarithm_scale=logarithm_scale, residual_input=residual_input, attention_head_outputs=attention_head_outputs, output_weight=output_weight, adapter_down_weight=adapter_down_weight, adapter_up_weight=adapter_up_weight, final_norm_weight=final_norm_weight, lengths=lengths)


grad_scale = 512.0
adapter_scale = 2.0
epsilon = 1e-05

def reference(query_embeddings, passage_embeddings, positives, logarithm_scale, residual_input, attention_head_outputs, output_weight, adapter_down_weight, adapter_up_weight, final_norm_weight, lengths):
    logit_scale = jnp.exp(logarithm_scale)
    logits = logit_scale * jnp.dot(query_embeddings, passage_embeddings.T, preferred_element_type=jnp.float32)
    row_max = lax.optimization_barrier(jnp.max(logits, axis=1))
    log_norm = row_max + jnp.log(lax.optimization_barrier(jnp.sum(jnp.exp(logits - row_max[:, None]), axis=1)))
    column = jnp.arange(B, dtype=jnp.int32)
    onehot = (column[None, :] == positives[:, None]).astype(jnp.float32)
    pos_logit = lax.optimization_barrier(jnp.sum(onehot * logits, axis=1))
    loss = jnp.mean(log_norm - pos_logit)
    weights = jnp.exp(logits - log_norm[:, None])
    scale_grad = jnp.mean(lax.optimization_barrier(jnp.sum(weights * logits, axis=1)) - pos_logit)
    weight_half = weights.astype(jnp.bfloat16)
    hot_half = onehot.astype(jnp.bfloat16)
    query_grad = logit_scale * (jnp.dot(weight_half, passage_embeddings, preferred_element_type=jnp.float32) - jnp.dot(hot_half, passage_embeddings, preferred_element_type=jnp.float32))
    passage_grad = logit_scale * (jnp.dot(weight_half.T, query_embeddings, preferred_element_type=jnp.float32) - jnp.dot(hot_half.T, query_embeddings, preferred_element_type=jnp.float32))
    row_grads = query_grad.reshape(B // Q_DEV, Q_DEV, MODEL_DIMENSION)[:, :ROWS_DEV].reshape(SEQS, MODEL_DIMENSION)
    position = jnp.arange(SEQ, dtype=jnp.int32)

    def per_sequence(carried_state, sequence_items):
        residual_vector_row, head_feature_row, row_grad, length = sequence_items
        projected_output = jnp.dot(head_feature_row, output_weight, preferred_element_type=jnp.float32)
        reduced_activation = jnp.dot(head_feature_row, adapter_down_weight, preferred_element_type=jnp.float32).astype(jnp.bfloat16)
        hidden_state = residual_vector_row.astype(jnp.float32) + projected_output + adapter_scale * jnp.dot(reduced_activation, adapter_up_weight, preferred_element_type=jnp.float32)
        inv_rms = lax.rsqrt(lax.optimization_barrier(jnp.mean(hidden_state * hidden_state, axis=1)) + epsilon)
        weight = grad_scale * (position < length).astype(jnp.float32) / length.astype(jnp.float32)
        gained = weight[:, None] * row_grad[None, :] * final_norm_weight[None, :]
        hidden_grad = inv_rms[:, None] * gained - hidden_state * (inv_rms * inv_rms * inv_rms * lax.optimization_barrier(jnp.mean(gained * hidden_state, axis=1)))[:, None]
        gradient_portion = hidden_grad.astype(jnp.bfloat16)
        reduced_gradient = (adapter_scale * jnp.dot(gradient_portion, adapter_up_weight.T, preferred_element_type=jnp.float32)).astype(jnp.bfloat16)
        head_gradient = (jnp.dot(gradient_portion, output_weight.T, preferred_element_type=jnp.float32) + jnp.dot(reduced_gradient, adapter_down_weight.T, preferred_element_type=jnp.float32)).astype(jnp.bfloat16)
        down_acc = carried_state[0] + jnp.dot(head_feature_row.T, reduced_gradient, preferred_element_type=jnp.float32)
        up_weight_accumulator = carried_state[1] + adapter_scale * jnp.dot(reduced_activation.T, gradient_portion, preferred_element_type=jnp.float32)
        return ((down_acc, up_weight_accumulator), (head_gradient, gradient_portion))
    initial = (jnp.zeros((HEAD_FEATURES, ADAPTER_RANK), jnp.float32), jnp.zeros((ADAPTER_RANK, MODEL_DIMENSION), jnp.float32))
    sums, grads = lax.scan(per_sequence, initial, (residual_input, attention_head_outputs, row_grads, lengths))
    return (loss, scale_grad, query_grad, passage_grad, grads[0], grads[1], sums[0] / SEQS, sums[1] / SEQS)
```

```python
import functools

import jax
import jax.numpy as jnp
from jax import lax
from jax.experimental import pallas as pl
from jax.experimental.pallas import tpu as pltpu
from jax.sharding import PartitionSpec as P

grad_scale = 512.0
adapter_scale = 2.0
epsilon = 1e-05
contract_rows = (((0,), (0,)), ((), ()))
contracted_columns = (((1,), (1,)), ((), ()))
MESH = pl.DeviceIdType.MESH
code_base = 256


def remote(src, dst, send, recv, target):
    return pltpu.make_async_remote_copy(
        src_ref=src, dst_ref=dst, send_sem=send, recv_sem=recv, device_id=target, device_id_type=MESH
    )


def greet(targets):
    barrier = pltpu.get_barrier_semaphore()
    for target in targets:
        pl.semaphore_signal(barrier, inc=1, device_id=target, device_id_type=MESH)
    pl.semaphore_wait(barrier, len(targets))


def gather_kernel(
    groups, shards, own_w, own_pair, w_all, pair_all,
    local_sem, z_send, z_recv, pz_send, pz_recv,
    ring_send, ring_recv, sib_send, sib_recv,
):
    g = lax.axis_index("group")
    f = lax.axis_index("fsdp")
    core = lax.rem(g, 2)
    chip = lax.div(g, 2)
    chips = groups // 2
    half_ring = chips // 2
    sibling = (g + 1 - 2 * core, f)
    column, line = lax.rem(chip, 2), lax.div(chip, 2)
    place = column * (chips - 1 - line) + (1 - column) * line
    rows = own_w.shape[0]
    part = rows // groups
    half = part // 2

    def member(position):
        position = lax.rem(position + 2 * chips, chips)
        back = lax.div(position, half_ring)
        where = (1 - back) * 2 * position + back * (2 * (chips - 1 - position) + 1)
        return 2 * where + core

    neighbours = ((member(place + 1), f), (member(place - 1), f))
    greet([(g, lax.rem(f + k, shards)) for k in range(1, shards)] + list(neighbours) + [sibling])

    def piece(block, owner):
        return w_all.at[pl.ds(pl.multiple_of(block * rows + owner * part, 16), part)]

    def half_piece(block, owner, way):
        return w_all.at[pl.ds(pl.multiple_of(block * rows + owner * part + way * half, 16), half)]

    def z_copy(k, side):
        step = 1 - 2 * side
        block = f - step * (k - 1)
        here = own_w.at[pl.ds(pl.multiple_of(g * part, 16), part)] if k == 1 else piece(block, g)
        there = (block >= 0) & (block < shards) & (f + step >= 0) & (f + step < shards)
        return there, remote(
            here, piece(block, g), z_send.at[side, k - 1], z_recv.at[side, k - 1], (g, f + step)
        )

    def z_start(k):
        for side in (0, 1):
            there, copy = z_copy(k, side)

            @pl.when(there)
            def _():
                copy.start()

    def z_wait(k):
        for side in (0, 1):
            block = f - (1 - 2 * side) * k

            @pl.when((block >= 0) & (block < shards))
            def _():
                remote(
                    piece(block, g), piece(block, g), z_send.at[side, k - 1], z_recv.at[side, k - 1], sibling
                ).wait_recv()

    z_start(1)
    keep_w = pltpu.make_async_copy(
        own_w, w_all.at[pl.ds(pl.multiple_of(f * rows, 16), rows)], local_sem.at[0]
    )
    keep_pair = pltpu.make_async_copy(own_pair, pair_all.at[g, f], local_sem.at[1])
    keep_pair.start()
    pair_copies = [
        remote(own_pair, pair_all.at[g, f], pz_send.at[k], pz_recv.at[k], (g, lax.rem(f + k, shards)))
        for k in range(1, shards)
    ]
    for copy in pair_copies:
        copy.start()
    keep_w.start()
    keep_pair.wait()
    for k in range(1, shards):
        source = lax.rem(f + shards - k, shards)
        remote(own_pair, pair_all.at[g, source], pz_send.at[k], pz_recv.at[k], sibling).wait_recv()

    def ring(slot, whole, halves):
        pieces = []
        own = remote(whole, whole, sib_send.at[slot, chips - 1, 0], sib_recv.at[slot, chips - 1, 0], sibling)
        own.start()
        for h in range(1, chips):
            for way in (0, 1):
                step = 1 - 2 * way
                src = halves(member(place - step * (h - 1)), way)
                remote(
                    src, src, ring_send.at[slot, h - 1, way], ring_recv.at[slot, h - 1, way], neighbours[way]
                ).start()
            for way in (0, 1):
                step = 1 - 2 * way
                got = halves(member(place - step * h), way)
                remote(
                    got, got, ring_send.at[slot, h - 1, way], ring_recv.at[slot, h - 1, way], neighbours[way]
                ).wait_recv()
                remote(
                    got, got, sib_send.at[slot, h - 1, way], sib_recv.at[slot, h - 1, way], sibling
                ).start()

    def ring_finish(slot, whole, halves, other_whole, other_halves):
        own = remote(whole, other_whole, sib_send.at[slot, chips - 1, 0], sib_recv.at[slot, chips - 1, 0], sibling)
        own.wait_send()
        own.wait_recv()
        for h in range(1, chips):
            for way in (0, 1):
                step = 1 - 2 * way
                sent = halves(member(place - step * (h - 1)), way)
                remote(
                    sent, sent, ring_send.at[slot, h - 1, way], ring_recv.at[slot, h - 1, way], neighbours[way]
                ).wait_send()
                got = halves(member(place - step * h), way)
                other = other_halves(member(place - step * h), way)
                handed = remote(
                    got, other, sib_send.at[slot, h - 1, way], sib_recv.at[slot, h - 1, way], sibling
                )
                handed.wait_send()
                handed.wait_recv()

    middle = shards // 2

    def pair_half(owner, way):
        return pair_all.at[owner, pl.ds(way * middle, middle)]

    def flip(owner):
        return owner + 1 - 2 * core

    ring(shards, pair_all.at[g], pair_half)

    def w_ring(block):
        ring(block, piece(block, g), lambda owner, way: half_piece(block, owner, way))

    def w_finish(block):
        ring_finish(
            block,
            piece(block, g),
            lambda owner, way: half_piece(block, owner, way),
            piece(block, flip(g)),
            lambda owner, way: half_piece(block, flip(owner), way),
        )

    def blocks(k):
        low = (f - k >= 0).astype(jnp.int32)
        high = (f + k < shards).astype(jnp.int32)
        first = low * (f - k) + (1 - low) * (f + k)
        return ((low + high > 0, first), (low + high > 1, f + k))

    z_wait(1)
    if shards > 2:
        z_start(2)
    for k in range(1, shards):
        first, second = blocks(k)

        @pl.when(first[0])
        def _():
            w_ring(first[1])

        if k + 1 < shards:
            z_wait(k + 1)
        if k + 2 < shards:
            z_start(k + 2)

        @pl.when(second[0])
        def _():
            w_ring(second[1])

    ring_finish(
        shards, pair_all.at[g], pair_half, pair_all.at[flip(g)], lambda owner, way: pair_half(flip(owner), way)
    )
    for k in range(1, shards):
        for there, block in blocks(k):

            @pl.when(there)
            def _():
                w_finish(block)

        for side in (0, 1):
            there, copy = z_copy(k, side)

            @pl.when(there)
            def _():
                copy.wait_send()

    for copy in pair_copies:
        copy.wait_send()
    keep_w.wait()


def gather_all(groups, shards, own_w, own_pair):
    rows, width = own_w.shape
    chips = groups // 2
    any_space = pl.BlockSpec(memory_space=pl.ANY)
    dma = pltpu.SemaphoreType.DMA
    return pl.pallas_call(
        functools.partial(gather_kernel, groups, shards),
        out_shape=(
            jax.ShapeDtypeStruct((shards * rows, width), own_w.dtype),
            jax.ShapeDtypeStruct((groups, shards) + own_pair.shape, own_pair.dtype),
        ),
        in_specs=[any_space, any_space],
        out_specs=(any_space, any_space),
        scratch_shapes=[
            dma((2,)),
            dma((2, shards)),
            dma((2, shards)),
            dma((shards,)),
            dma((shards,)),
            dma((shards + 1, chips, 2)),
            dma((shards + 1, chips, 2)),
            dma((shards + 1, chips, 2)),
            dma((shards + 1, chips, 2)),
        ],
        compiler_params=pltpu.CompilerParams(collective_id=0, has_side_effects=True),
        name="gather_all",
    )(own_w, own_pair)


def sum_kernel(groups, shards, part, out, in_group, in_shard, mine, total, sem_send, sem_recv):
    g = lax.axis_index("group")
    f = lax.axis_index("fsdp")
    group_to = [(lax.rem(g + k, groups), f) for k in range(1, groups)]
    shard_to = [(g, lax.rem(f + k, shards)) for k in range(1, shards)]
    greet(group_to + shard_to)

    def stage(index, copies):
        for copy in copies:
            copy.start()
        return copies

    first = stage(0, [
        remote(part.at[group_to[k - 1][0]], in_group.at[k], sem_send.at[0, k], sem_recv.at[0, k], group_to[k - 1])
        for k in range(1, groups)
    ])
    total_here = part[g]
    for k, copy in enumerate(first):
        copy.wait_recv()
        total_here = total_here + in_group[k + 1]
    mine[...] = total_here
    second = stage(1, [
        remote(mine.at[shard_to[k - 1][1]], in_shard.at[k], sem_send.at[1, k], sem_recv.at[1, k], shard_to[k - 1])
        for k in range(1, shards)
    ])
    total_here = mine[f]
    for k, copy in enumerate(second):
        copy.wait_recv()
        total_here = total_here + in_shard[k + 1]
    total[g, f] = total_here
    third = stage(2, [
        remote(total.at[g, f], total.at[g, f], sem_send.at[2, k], sem_recv.at[2, k], shard_to[k - 1])
        for k in range(1, shards)
    ])
    for k in range(1, shards):
        source = lax.rem(f + shards - k, shards)
        remote(
            total.at[g, f], total.at[g, source], sem_send.at[2, k], sem_recv.at[2, k], shard_to[k - 1]
        ).wait_recv()
    fourth = stage(3, [
        remote(total.at[g], total.at[g], sem_send.at[3, k], sem_recv.at[3, k], group_to[k - 1])
        for k in range(1, groups)
    ])
    for k in range(1, groups):
        source = lax.rem(g + groups - k, groups)
        remote(
            total.at[g], total.at[source], sem_send.at[3, k], sem_recv.at[3, k], group_to[k - 1]
        ).wait_recv()
    out[...] = total[...]
    for copy in first + second + third + fourth:
        copy.wait_send()


def sum_all(groups, shards, part):
    rows, lanes = part.shape[2:]
    vmem = pl.BlockSpec(memory_space=pltpu.VMEM)
    most = max(groups, shards)
    return pl.pallas_call(
        functools.partial(sum_kernel, groups, shards),
        out_shape=jax.ShapeDtypeStruct(part.shape, part.dtype),
        in_specs=[vmem],
        out_specs=vmem,
        scratch_shapes=[
            pltpu.VMEM((groups, shards, rows, lanes), part.dtype),
            pltpu.VMEM((shards, rows, lanes), part.dtype),
            pltpu.VMEM((shards, rows, lanes), part.dtype),
            pltpu.VMEM(part.shape, part.dtype),
            pltpu.SemaphoreType.DMA((4, most)),
            pltpu.SemaphoreType.DMA((4, most)),
        ],
        compiler_params=pltpu.CompilerParams(collective_id=1, has_side_effects=True),
        name="sum_all",
    )(part)


def on_device(
    groups,
    shards,
    query_embeddings,
    passage_embeddings,
    positives,
    logarithm_scale,
    residual_input,
    attention_head_outputs,
    output_weight,
    adapter_down_weight,
    adapter_up_weight,
    final_norm_weight,
    lengths,
):
    device_count = groups * shards
    own_index = lax.axis_index(("group", "fsdp"))
    q_count, model_width = query_embeddings.shape
    total_queries = q_count * device_count
    logit_scale = jnp.exp(logarithm_scale)
    seq_here, seq_len, _ = residual_input.shape
    heads_width = attention_head_outputs.shape[2]
    rank = adapter_up_weight.shape[0]
    token_rows = attention_head_outputs.reshape(-1, heads_width)

    packed_width = q_count * model_width // 8
    code = jnp.concatenate([positives // code_base, positives % code_base]).astype(jnp.bfloat16)
    code = jnp.broadcast_to(jnp.pad(code, (0, 128 - 2 * q_count))[None, :], (16, 128))
    own_pair = jnp.concatenate(
        [
            jnp.concatenate(
                [query_embeddings.reshape(8, packed_width), passage_embeddings.reshape(8, packed_width)], axis=0
            ),
            code,
        ],
        axis=1,
    )
    full_weight, pairs = gather_all(groups, shards, output_weight, own_pair)
    pairs = pairs.reshape(device_count, 16, packed_width + 128)
    queries = pairs[:, :8, :packed_width].reshape(total_queries, model_width)
    passages = pairs[:, 8:, :packed_width].reshape(total_queries, model_width)
    codes = pairs[:, 0, packed_width : packed_width + 2 * q_count].astype(jnp.int32)
    pos_all = (codes[:, :q_count] * code_base + codes[:, q_count:]).reshape(total_queries)

    logits = logit_scale * lax.dot_general(
        queries, passages, contracted_columns, preferred_element_type=jnp.float32
    )
    hits = jnp.arange(total_queries, dtype=jnp.int32)[None, :] == pos_all[:, None]
    row_max = jnp.max(logits, axis=1)
    log_norm = row_max + jnp.log(jnp.sum(jnp.exp(logits - row_max[:, None]), axis=1))
    pos_logit = jnp.sum(jnp.where(hits, logits, 0.0), axis=1)
    weights = jnp.exp(logits - log_norm[:, None])
    loss = jnp.mean(log_norm - pos_logit)
    scale_grad = jnp.mean(jnp.sum(weights * logits, axis=1) - pos_logit)
    weight_half = weights.astype(jnp.bfloat16)
    hot_half = hits.astype(jnp.bfloat16)
    first_own = own_index * q_count
    own_rows = jnp.concatenate(
        [
            lax.dynamic_slice_in_dim(weight_half, first_own, q_count, 0),
            lax.dynamic_slice_in_dim(hot_half, first_own, q_count, 0),
        ],
        axis=0,
    )
    own_columns = jnp.concatenate(
        [
            lax.dynamic_slice_in_dim(weight_half, first_own, q_count, 1),
            lax.dynamic_slice_in_dim(hot_half, first_own, q_count, 1),
        ],
        axis=1,
    )
    by_query = jnp.dot(own_rows, passages, preferred_element_type=jnp.float32)
    query_grad = logit_scale * (by_query[:q_count] - by_query[q_count:])
    by_passage = lax.dot_general(own_columns, queries, contract_rows, preferred_element_type=jnp.float32)
    passage_grad = logit_scale * (by_passage[:q_count] - by_passage[q_count:])

    reduced_activation = jnp.dot(
        token_rows, adapter_down_weight, preferred_element_type=jnp.float32
    ).astype(jnp.bfloat16)
    hidden_state = (
        residual_input.reshape(-1, model_width).astype(jnp.float32)
        + jnp.dot(token_rows, full_weight, preferred_element_type=jnp.float32)
        + adapter_scale
        * jnp.dot(reduced_activation, adapter_up_weight, preferred_element_type=jnp.float32)
    )
    row_grads = query_grad[:seq_here]
    position = jnp.arange(seq_len, dtype=jnp.int32)
    weight = (
        grad_scale
        * (position[None, :] < lengths[:, None]).astype(jnp.float32)
        / lengths[:, None].astype(jnp.float32)
    )
    gained = (
        weight[:, :, None] * row_grads[:, None, :] * final_norm_weight[None, None, :]
    ).reshape(-1, model_width)
    inv_rms = lax.rsqrt(jnp.mean(hidden_state * hidden_state, axis=1) + epsilon)
    hidden_grad = (
        inv_rms[:, None] * gained
        - hidden_state
        * (inv_rms * inv_rms * inv_rms * jnp.mean(gained * hidden_state, axis=1))[:, None]
    )
    gradient_portion = hidden_grad.astype(jnp.bfloat16)
    reduced_gradient = (
        adapter_scale
        * lax.dot_general(
            gradient_portion,
            adapter_up_weight,
            contracted_columns,
            preferred_element_type=jnp.float32,
        )
    ).astype(jnp.bfloat16)
    down_part = lax.dot_general(
        reduced_gradient, token_rows, contract_rows, preferred_element_type=jnp.float32
    )
    up_part = adapter_scale * lax.dot_general(
        reduced_activation, gradient_portion, contract_rows, preferred_element_type=jnp.float32
    )
    both = jnp.concatenate([down_part.reshape(-1, 128), up_part.reshape(-1, 128)], axis=0)
    summed = sum_all(groups, shards, both.reshape(groups, shards, -1, 128)).reshape(-1, 128)
    summed = summed / (seq_here * device_count)
    down_rows = rank * heads_width // 128
    down_total = summed[:down_rows].reshape(rank, heads_width).T
    up_total = summed[down_rows:].reshape(rank, model_width)
    head_gradient = (
        lax.dot_general(
            gradient_portion, full_weight, contracted_columns, preferred_element_type=jnp.float32
        )
        + lax.dot_general(
            reduced_gradient,
            adapter_down_weight,
            contracted_columns,
            preferred_element_type=jnp.float32,
        )
    ).astype(jnp.bfloat16)
    return (
        loss,
        scale_grad,
        query_grad,
        passage_grad,
        head_gradient.reshape(seq_here, seq_len, heads_width),
        gradient_portion.reshape(seq_here, seq_len, model_width),
        down_total,
        up_total,
    )


def solution(mesh):
    both = ("group", "fsdp")
    placed = (
        P(both, None),
        P(both, None),
        P(both),
        P(),
        P(both, None, None),
        P(both, None, None),
        P("fsdp", None),
        P(),
        P(),
        P(),
        P(both),
    )
    return jax.shard_map(
        functools.partial(on_device, mesh.shape["group"], mesh.shape["fsdp"]),
        mesh=mesh,
        in_specs=placed,
        out_specs=(
            P(),
            P(),
            P(both, None),
            P(both, None),
            P(both, None, None),
            P(both, None, None),
            P(),
            P(),
        ),
        check_vma=False,
    )
```

```python
import functools

import jax
import jax.numpy as jnp
from jax import lax
from jax.experimental import pallas as pl
from jax.experimental.pallas import tpu as pltpu
from jax.sharding import PartitionSpec as P

grad_scale = 512.0
adapter_scale = 2.0
epsilon = 1e-05
contract_rows = (((0,), (0,)), ((), ()))
contracted_columns = (((1,), (1,)), ((), ()))
MESH = pl.DeviceIdType.MESH
code_base = 256


def remote(src, dst, send, recv, target):
    return pltpu.make_async_remote_copy(
        src_ref=src, dst_ref=dst, send_sem=send, recv_sem=recv, device_id=target, device_id_type=MESH
    )


def greet(targets):
    barrier = pltpu.get_barrier_semaphore()
    for target in targets:
        pl.semaphore_signal(barrier, inc=1, device_id=target, device_id_type=MESH)
    pl.semaphore_wait(barrier, len(targets))


def gather_kernel(
    groups, shards, own_w, own_pair, w_all, pair_all,
    local_sem, z_send, z_recv, pz_send, pz_recv,
    ring_send, ring_recv, sib_send, sib_recv, staged,
):
    g = lax.axis_index("group")
    f = lax.axis_index("fsdp")
    core = lax.rem(g, 2)
    chip = lax.div(g, 2)
    chips = groups // 2
    half_ring = chips // 2
    sibling = (g + 1 - 2 * core, f)
    column, line = lax.rem(chip, 2), lax.div(chip, 2)
    place = column * (chips - 1 - line) + (1 - column) * line
    rows = own_w.shape[0]
    part = rows // groups
    half = part // 2

    def member(position):
        position = lax.rem(position + 2 * chips, chips)
        back = lax.div(position, half_ring)
        where = (1 - back) * 2 * position + back * (2 * (chips - 1 - position) + 1)
        return 2 * where + core

    neighbours = ((member(place + 1), f), (member(place - 1), f))
    greet([(g, lax.rem(f + k, shards)) for k in range(1, shards)] + list(neighbours) + [sibling])

    def piece(block, owner):
        return w_all.at[pl.ds(pl.multiple_of(block * rows + owner * part, 16), part)]

    def half_piece(block, owner, way):
        return w_all.at[pl.ds(pl.multiple_of(block * rows + owner * part + way * half, 16), half)]

    def quarter(block, owner, way, sub):
        columns = own_w.shape[1] // 2
        return w_all.at[
            pl.ds(pl.multiple_of(block * rows + owner * part + way * half, 16), half),
            pl.ds(sub * columns, columns),
        ]

    last = shards - 1
    near = jnp.minimum(f, last - f)
    tied = jnp.minimum(near, 1)

    def order(j):
        paired = (j < 2 * near).astype(jnp.int32)
        far_side = (f < last - f).astype(jnp.int32)
        hop = paired * (lax.div(j, 2) + 1) + (1 - paired) * (near + 1 + j - 2 * near)
        side = paired * lax.rem(j, 2) + (1 - paired) * far_side
        return hop, side, f - (1 - 2 * side) * hop

    def z_copy(src, block, hop, side):
        step = 1 - 2 * side
        return remote(
            src, piece(block, g), z_send.at[side, hop - 1], z_recv.at[side, hop - 1], (g, f + step)
        )

    def on_line(side):
        onward = f + 1 - 2 * side
        return (onward >= 0) & (onward < shards)

    def arrive(j):
        hop, side, block = order(j)
        z_copy(piece(block, g), block, hop, side).wait_recv()

        @pl.when(on_line(side))
        def _():
            z_copy(piece(block, g), block, hop + 1, side).start()

    pair_copies = [
        remote(own_pair, pair_all.at[g, f], pz_send.at[k], pz_recv.at[k], (g, lax.rem(f + k, shards)))
        for k in range(1, shards)
    ]
    for copy in pair_copies:
        copy.start()
    keep_pair = pltpu.make_async_copy(own_pair, pair_all.at[g, f], local_sem.at[1])
    keep_pair.start()
    own_part = own_w.at[pl.ds(pl.multiple_of(g * part, 16), part)]
    for side in (0, 1):

        @pl.when(on_line(side))
        def _():
            z_copy(own_part, f, 1, side).start()

    stage = pltpu.make_async_copy(own_w, staged, local_sem.at[0])
    stage.start()
    keep_pair.wait()
    for k in range(1, shards):
        source = lax.rem(f + shards - k, shards)
        remote(own_pair, pair_all.at[g, source], pz_send.at[k], pz_recv.at[k], sibling).wait_recv()

    def ring_copy(slot, h, way, sub, ref):
        at = 2 * way + sub
        return remote(ref, ref, ring_send.at[slot, h - 1, at], ring_recv.at[slot, h - 1, at], neighbours[way])

    def from_behind(way, h):
        return member(place - (1 - 2 * way) * h)

    def own_hand(slot, whole, other):
        return remote(whole, other, sib_send.at[slot, chips - 1, 0], sib_recv.at[slot, chips - 1, 0], sibling)

    def ring_start(slot, whole, cut, subs):
        for sub in range(subs):
            for way in (0, 1):
                ring_copy(slot, 1, way, sub, cut(from_behind(way, 0), way, sub)).start()
        own_hand(slot, whole, whole).start()

    def ring(slot, cut, subs, halves, late):
        for h in range(1, chips):
            if h == chips - 1:
                late()
            for sub in range(subs):
                for way in (0, 1):
                    got = cut(from_behind(way, h), way, sub)
                    ring_copy(slot, h, way, sub, got).wait_recv()
                    if h < chips - 1:
                        ring_copy(slot, h + 1, way, sub, got).start()
            for way in (0, 1):
                got = halves(from_behind(way, h), way)
                remote(
                    got, got, sib_send.at[slot, h - 1, way], sib_recv.at[slot, h - 1, way], sibling
                ).start()

    def ring_finish(slot, whole, cut, subs, halves, other_whole, other_halves):
        own = own_hand(slot, whole, other_whole)
        own.wait_send()
        own.wait_recv()
        for h in range(1, chips):
            for way in (0, 1):
                for sub in range(subs):
                    ring_copy(slot, h, way, sub, cut(from_behind(way, h - 1), way, sub)).wait_send()
                got = halves(from_behind(way, h), way)
                other = other_halves(from_behind(way, h), way)
                handed = remote(
                    got, other, sib_send.at[slot, h - 1, way], sib_recv.at[slot, h - 1, way], sibling
                )
                handed.wait_send()
                handed.wait_recv()

    middle = shards // 2

    def pair_half(owner, way, sub=0):
        return pair_all.at[owner, pl.ds(way * middle, middle)]

    def flip(owner):
        return owner + 1 - 2 * core

    def w_start(j):
        _, _, block = order(j)
        ring_start(block, piece(block, g), functools.partial(quarter, block), 2)

    ring_start(shards, pair_all.at[g], pair_half, 1)
    ring(shards, pair_half, 1, pair_half, lambda: None)
    stage.wait()
    keep_w = pltpu.make_async_copy(
        staged, w_all.at[pl.ds(pl.multiple_of(f * rows, 16), rows)], local_sem.at[0]
    )
    keep_w.start()
    arrive(0)
    if last > 1:

        @pl.when(tied > 0)
        def _():
            arrive(1)

    w_start(0)
    for j in range(last):
        def late():
            @pl.when(j + 1 + tied < last)
            def _():
                arrive(j + 1 + tied)

            if j + 1 < last:
                w_start(j + 1)

        _, _, block = order(j)
        ring(block, functools.partial(quarter, block), 2, functools.partial(half_piece, block), late)

    ring_finish(
        shards, pair_all.at[g], pair_half, 1, pair_half, pair_all.at[flip(g)],
        lambda owner, way: pair_half(flip(owner), way),
    )
    for side in (0, 1):

        @pl.when(on_line(side))
        def _():
            z_copy(own_part, f, 1, side).wait_send()

    for j in range(last):
        hop, side, block = order(j)
        ring_finish(
            block, piece(block, g), functools.partial(quarter, block), 2, functools.partial(half_piece, block),
            piece(block, flip(g)), lambda owner, way: half_piece(block, flip(owner), way),
        )

        @pl.when(on_line(side))
        def _():
            z_copy(piece(block, g), block, hop + 1, side).wait_send()

    for copy in pair_copies:
        copy.wait_send()
    keep_w.wait()


def gather_all(groups, shards, own_w, own_pair):
    rows, width = own_w.shape
    chips = groups // 2
    any_space = pl.BlockSpec(memory_space=pl.ANY)
    dma = pltpu.SemaphoreType.DMA
    return pl.pallas_call(
        functools.partial(gather_kernel, groups, shards),
        out_shape=(
            jax.ShapeDtypeStruct((shards * rows, width), own_w.dtype),
            jax.ShapeDtypeStruct((groups, shards) + own_pair.shape, own_pair.dtype),
        ),
        in_specs=[any_space, any_space],
        out_specs=(any_space, any_space),
        scratch_shapes=[
            dma((2,)),
            dma((2, shards)),
            dma((2, shards)),
            dma((shards,)),
            dma((shards,)),
            dma((shards + 1, chips, 4)),
            dma((shards + 1, chips, 4)),
            dma((shards + 1, chips, 2)),
            dma((shards + 1, chips, 2)),
            pltpu.VMEM(own_w.shape, own_w.dtype),
        ],
        compiler_params=pltpu.CompilerParams(
            collective_id=0,
            has_side_effects=True,
            vmem_limit_bytes=own_w.size * own_w.dtype.itemsize + (8 << 20),
        ),
        name="gather_all",
    )(own_w, own_pair)


def sum_kernel(groups, shards, part, out, in_group, in_shard, mine, total, sem_send, sem_recv):
    g = lax.axis_index("group")
    f = lax.axis_index("fsdp")
    group_to = [(lax.rem(g + k, groups), f) for k in range(1, groups)]
    shard_to = [(g, lax.rem(f + k, shards)) for k in range(1, shards)]
    greet(group_to + shard_to)

    def stage(index, copies):
        for copy in copies:
            copy.start()
        return copies

    first = stage(0, [
        remote(part.at[group_to[k - 1][0]], in_group.at[k], sem_send.at[0, k], sem_recv.at[0, k], group_to[k - 1])
        for k in range(1, groups)
    ])
    total_here = part[g]
    for k, copy in enumerate(first):
        copy.wait_recv()
        total_here = total_here + in_group[k + 1]
    mine[...] = total_here
    second = stage(1, [
        remote(mine.at[shard_to[k - 1][1]], in_shard.at[k], sem_send.at[1, k], sem_recv.at[1, k], shard_to[k - 1])
        for k in range(1, shards)
    ])
    total_here = mine[f]
    for k, copy in enumerate(second):
        copy.wait_recv()
        total_here = total_here + in_shard[k + 1]
    total[g, f] = total_here
    third = stage(2, [
        remote(total.at[g, f], total.at[g, f], sem_send.at[2, k], sem_recv.at[2, k], shard_to[k - 1])
        for k in range(1, shards)
    ])
    for k in range(1, shards):
        source = lax.rem(f + shards - k, shards)
        remote(
            total.at[g, f], total.at[g, source], sem_send.at[2, k], sem_recv.at[2, k], shard_to[k - 1]
        ).wait_recv()
    fourth = stage(3, [
        remote(total.at[g], total.at[g], sem_send.at[3, k], sem_recv.at[3, k], group_to[k - 1])
        for k in range(1, groups)
    ])
    for k in range(1, groups):
        source = lax.rem(g + groups - k, groups)
        remote(
            total.at[g], total.at[source], sem_send.at[3, k], sem_recv.at[3, k], group_to[k - 1]
        ).wait_recv()
    out[...] = total[...]
    for copy in first + second + third + fourth:
        copy.wait_send()


def sum_all(groups, shards, part):
    rows, lanes = part.shape[2:]
    vmem = pl.BlockSpec(memory_space=pltpu.VMEM)
    most = max(groups, shards)
    return pl.pallas_call(
        functools.partial(sum_kernel, groups, shards),
        out_shape=jax.ShapeDtypeStruct(part.shape, part.dtype),
        in_specs=[vmem],
        out_specs=vmem,
        scratch_shapes=[
            pltpu.VMEM((groups, shards, rows, lanes), part.dtype),
            pltpu.VMEM((shards, rows, lanes), part.dtype),
            pltpu.VMEM((shards, rows, lanes), part.dtype),
            pltpu.VMEM(part.shape, part.dtype),
            pltpu.SemaphoreType.DMA((4, most)),
            pltpu.SemaphoreType.DMA((4, most)),
        ],
        compiler_params=pltpu.CompilerParams(collective_id=1, has_side_effects=True),
        name="sum_all",
    )(part)


def on_device(
    groups,
    shards,
    query_embeddings,
    passage_embeddings,
    positives,
    logarithm_scale,
    residual_input,
    attention_head_outputs,
    output_weight,
    adapter_down_weight,
    adapter_up_weight,
    final_norm_weight,
    lengths,
):
    device_count = groups * shards
    own_index = lax.axis_index(("group", "fsdp"))
    q_count, model_width = query_embeddings.shape
    total_queries = q_count * device_count
    logit_scale = jnp.exp(logarithm_scale)
    seq_here, seq_len, _ = residual_input.shape
    heads_width = attention_head_outputs.shape[2]
    rank = adapter_up_weight.shape[0]
    token_rows = attention_head_outputs.reshape(-1, heads_width)

    packed_width = q_count * model_width // 8
    code = jnp.concatenate([positives // code_base, positives % code_base]).astype(jnp.bfloat16)
    code = jnp.broadcast_to(jnp.pad(code, (0, 128 - 2 * q_count))[None, :], (16, 128))
    own_pair = jnp.concatenate(
        [
            jnp.concatenate(
                [query_embeddings.reshape(8, packed_width), passage_embeddings.reshape(8, packed_width)], axis=0
            ),
            code,
        ],
        axis=1,
    )
    full_weight, pairs = gather_all(groups, shards, output_weight, own_pair)
    pairs = pairs.reshape(device_count, 16, packed_width + 128)
    queries = pairs[:, :8, :packed_width].reshape(total_queries, model_width)
    passages = pairs[:, 8:, :packed_width].reshape(total_queries, model_width)
    codes = pairs[:, 0, packed_width : packed_width + 2 * q_count].astype(jnp.int32)
    pos_all = (codes[:, :q_count] * code_base + codes[:, q_count:]).reshape(total_queries)

    logits = logit_scale * lax.dot_general(
        queries, passages, contracted_columns, preferred_element_type=jnp.float32
    )
    hits = jnp.arange(total_queries, dtype=jnp.int32)[None, :] == pos_all[:, None]
    row_max = jnp.max(logits, axis=1)
    log_norm = row_max + jnp.log(jnp.sum(jnp.exp(logits - row_max[:, None]), axis=1))
    pos_logit = jnp.sum(jnp.where(hits, logits, 0.0), axis=1)
    weights = jnp.exp(logits - log_norm[:, None])
    loss = jnp.mean(log_norm - pos_logit)
    scale_grad = jnp.mean(jnp.sum(weights * logits, axis=1) - pos_logit)
    weight_half = weights.astype(jnp.bfloat16)
    hot_half = hits.astype(jnp.bfloat16)
    first_own = own_index * q_count
    own_rows = jnp.concatenate(
        [
            lax.dynamic_slice_in_dim(weight_half, first_own, q_count, 0),
            lax.dynamic_slice_in_dim(hot_half, first_own, q_count, 0),
        ],
        axis=0,
    )
    own_columns = jnp.concatenate(
        [
            lax.dynamic_slice_in_dim(weight_half, first_own, q_count, 1),
            lax.dynamic_slice_in_dim(hot_half, first_own, q_count, 1),
        ],
        axis=1,
    )
    by_query = jnp.dot(own_rows, passages, preferred_element_type=jnp.float32)
    query_grad = logit_scale * (by_query[:q_count] - by_query[q_count:])
    by_passage = lax.dot_general(own_columns, queries, contract_rows, preferred_element_type=jnp.float32)
    passage_grad = logit_scale * (by_passage[:q_count] - by_passage[q_count:])

    reduced_activation = jnp.dot(
        token_rows, adapter_down_weight, preferred_element_type=jnp.float32
    ).astype(jnp.bfloat16)
    hidden_state = (
        residual_input.reshape(-1, model_width).astype(jnp.float32)
        + jnp.dot(token_rows, full_weight, preferred_element_type=jnp.float32)
        + adapter_scale
        * jnp.dot(reduced_activation, adapter_up_weight, preferred_element_type=jnp.float32)
    )
    row_grads = query_grad[:seq_here]
    position = jnp.arange(seq_len, dtype=jnp.int32)
    weight = (
        grad_scale
        * (position[None, :] < lengths[:, None]).astype(jnp.float32)
        / lengths[:, None].astype(jnp.float32)
    )
    gained = (
        weight[:, :, None] * row_grads[:, None, :] * final_norm_weight[None, None, :]
    ).reshape(-1, model_width)
    inv_rms = lax.rsqrt(jnp.mean(hidden_state * hidden_state, axis=1) + epsilon)
    hidden_grad = (
        inv_rms[:, None] * gained
        - hidden_state
        * (inv_rms * inv_rms * inv_rms * jnp.mean(gained * hidden_state, axis=1))[:, None]
    )
    gradient_portion = hidden_grad.astype(jnp.bfloat16)
    reduced_gradient = (
        adapter_scale
        * lax.dot_general(
            gradient_portion,
            adapter_up_weight,
            contracted_columns,
            preferred_element_type=jnp.float32,
        )
    ).astype(jnp.bfloat16)
    down_part = lax.dot_general(
        reduced_gradient, token_rows, contract_rows, preferred_element_type=jnp.float32
    )
    up_part = adapter_scale * lax.dot_general(
        reduced_activation, gradient_portion, contract_rows, preferred_element_type=jnp.float32
    )
    both = jnp.concatenate([down_part.reshape(-1, 128), up_part.reshape(-1, 128)], axis=0)
    summed = sum_all(groups, shards, both.reshape(groups, shards, -1, 128)).reshape(-1, 128)
    summed = summed / (seq_here * device_count)
    down_rows = rank * heads_width // 128
    down_total = summed[:down_rows].reshape(rank, heads_width).T
    up_total = summed[down_rows:].reshape(rank, model_width)
    head_gradient = (
        lax.dot_general(
            gradient_portion, full_weight, contracted_columns, preferred_element_type=jnp.float32
        )
        + lax.dot_general(
            reduced_gradient,
            adapter_down_weight,
            contracted_columns,
            preferred_element_type=jnp.float32,
        )
    ).astype(jnp.bfloat16)
    return (
        loss,
        scale_grad,
        query_grad,
        passage_grad,
        head_gradient.reshape(seq_here, seq_len, heads_width),
        gradient_portion.reshape(seq_here, seq_len, model_width),
        down_total,
        up_total,
    )


def solution(mesh):
    both = ("group", "fsdp")
    placed = (
        P(both, None),
        P(both, None),
        P(both),
        P(),
        P(both, None, None),
        P(both, None, None),
        P("fsdp", None),
        P(),
        P(),
        P(),
        P(both),
    )
    return jax.shard_map(
        functools.partial(on_device, mesh.shape["group"], mesh.shape["fsdp"]),
        mesh=mesh,
        in_specs=placed,
        out_specs=(
            P(),
            P(),
            P(both, None),
            P(both, None),
            P(both, None, None),
            P(both, None, None),
            P(),
            P(),
        ),
        check_vma=False,
    )
```

```python
import functools

import jax
import jax.numpy as jnp
from jax import lax
from jax.experimental import pallas as pl
from jax.experimental.pallas import tpu as pltpu
from jax.sharding import PartitionSpec as P

grad_scale = 512.0
adapter_scale = 2.0
epsilon = 1e-05
contract_rows = (((0,), (0,)), ((), ()))
contracted_columns = (((1,), (1,)), ((), ()))
MESH = pl.DeviceIdType.MESH
code_base = 256


def remote(src, dst, send, recv, target):
    return pltpu.make_async_remote_copy(
        src_ref=src, dst_ref=dst, send_sem=send, recv_sem=recv, device_id=target, device_id_type=MESH
    )


def greet(targets):
    barrier = pltpu.get_barrier_semaphore()
    for target in targets:
        pl.semaphore_signal(barrier, inc=1, device_id=target, device_id_type=MESH)
    pl.semaphore_wait(barrier, len(targets))


def gather_kernel(
    groups, shards, own_w, own_pair, w_all, pair_all,
    local_sem, z_send, z_recv, pz_send, pz_recv,
    ring_send, ring_recv, sib_send, sib_recv, staged,
):
    g = lax.axis_index("group")
    f = lax.axis_index("fsdp")
    core = lax.rem(g, 2)
    chip = lax.div(g, 2)
    chips = groups // 2
    half_ring = chips // 2
    sibling = (g + 1 - 2 * core, f)
    column, line = lax.rem(chip, 2), lax.div(chip, 2)
    place = column * (chips - 1 - line) + (1 - column) * line
    rows = own_w.shape[0]
    part = rows // groups
    half = part // 2

    def member(position):
        position = lax.rem(position + 2 * chips, chips)
        back = lax.div(position, half_ring)
        where = (1 - back) * 2 * position + back * (2 * (chips - 1 - position) + 1)
        return 2 * where + core

    neighbours = ((member(place + 1), f), (member(place - 1), f))
    greet([(g, lax.rem(f + k, shards)) for k in range(1, shards)] + list(neighbours) + [sibling])

    def piece(block, owner):
        return w_all.at[pl.ds(pl.multiple_of(block * rows + owner * part, 16), part)]

    def half_piece(block, owner, way):
        return w_all.at[pl.ds(pl.multiple_of(block * rows + owner * part + way * half, 16), half)]

    def quarter(block, owner, way, sub):
        columns = own_w.shape[1] // 2
        return w_all.at[
            pl.ds(pl.multiple_of(block * rows + owner * part + way * half, 16), half),
            pl.ds(sub * columns, columns),
        ]

    last = shards - 1
    near = jnp.minimum(f, last - f)
    tied = jnp.minimum(near, 1)

    def order(j):
        paired = (j < 2 * near).astype(jnp.int32)
        far_side = (f < last - f).astype(jnp.int32)
        hop = paired * (lax.div(j, 2) + 1) + (1 - paired) * (near + 1 + j - 2 * near)
        side = paired * lax.rem(j, 2) + (1 - paired) * far_side
        return hop, side, f - (1 - 2 * side) * hop

    def z_piece(block, sub):
        columns = own_w.shape[1] // 2
        return w_all.at[
            pl.ds(pl.multiple_of(block * rows + g * part, 16), part), pl.ds(sub * columns, columns)
        ]

    def z_copy(src, block, hop, side, sub):
        step = 1 - 2 * side
        at = 2 * (hop - 1) + sub
        return remote(
            src, z_piece(block, sub), z_send.at[side, at], z_recv.at[side, at], (g, f + step)
        )

    def on_line(side):
        onward = f + 1 - 2 * side
        return (onward >= 0) & (onward < shards)

    def arrive(j, sub):
        hop, side, block = order(j)
        z_copy(z_piece(block, sub), block, hop, side, sub).wait_recv()

        @pl.when(on_line(side))
        def _():
            z_copy(z_piece(block, sub), block, hop + 1, side, sub).start()

    pair_copies = [
        remote(own_pair, pair_all.at[g, f], pz_send.at[k], pz_recv.at[k], (g, lax.rem(f + k, shards)))
        for k in range(1, shards)
    ]
    for copy in pair_copies:
        copy.start()
    keep_pair = pltpu.make_async_copy(own_pair, pair_all.at[g, f], local_sem.at[1])
    keep_pair.start()

    def own_part(sub):
        columns = own_w.shape[1] // 2
        return own_w.at[pl.ds(pl.multiple_of(g * part, 16), part), pl.ds(sub * columns, columns)]

    def z_first(sub):
        for side in (0, 1):

            @pl.when(on_line(side))
            def _():
                z_copy(own_part(sub), f, 1, side, sub).start()

    z_first(0)
    stage = pltpu.make_async_copy(own_w, staged, local_sem.at[0])
    stage.start()
    keep_pair.wait()
    for k in range(1, shards):
        source = lax.rem(f + shards - k, shards)
        remote(own_pair, pair_all.at[g, source], pz_send.at[k], pz_recv.at[k], sibling).wait_recv()

    z_first(1)

    def ring_copy(slot, h, way, sub, ref):
        at = 2 * way + sub
        return remote(ref, ref, ring_send.at[slot, h - 1, at], ring_recv.at[slot, h - 1, at], neighbours[way])

    def from_behind(way, h):
        return member(place - (1 - 2 * way) * h)

    def own_hand(slot, whole, other):
        return remote(whole, other, sib_send.at[slot, chips - 1, 0], sib_recv.at[slot, chips - 1, 0], sibling)

    def ring_start(slot, whole, cut, subs, ready=lambda sub: None):
        for sub in range(subs):
            ready(sub)
            for way in (0, 1):
                ring_copy(slot, 1, way, sub, cut(from_behind(way, 0), way, sub)).start()
        own_hand(slot, whole, whole).start()

    def ring(slot, cut, subs, halves, late):
        for h in range(1, chips):
            if h == chips - 1:
                late()
            for sub in range(subs):
                for way in (0, 1):
                    got = cut(from_behind(way, h), way, sub)
                    ring_copy(slot, h, way, sub, got).wait_recv()
                    if h < chips - 1:
                        ring_copy(slot, h + 1, way, sub, got).start()
            for way in (0, 1):
                got = halves(from_behind(way, h), way)
                remote(
                    got, got, sib_send.at[slot, h - 1, way], sib_recv.at[slot, h - 1, way], sibling
                ).start()

    def ring_finish(slot, whole, cut, subs, halves, other_whole, other_halves):
        own = own_hand(slot, whole, other_whole)
        own.wait_send()
        own.wait_recv()
        for h in range(1, chips):
            for way in (0, 1):
                for sub in range(subs):
                    ring_copy(slot, h, way, sub, cut(from_behind(way, h - 1), way, sub)).wait_send()
                got = halves(from_behind(way, h), way)
                other = other_halves(from_behind(way, h), way)
                handed = remote(
                    got, other, sib_send.at[slot, h - 1, way], sib_recv.at[slot, h - 1, way], sibling
                )
                handed.wait_send()
                handed.wait_recv()

    middle = shards // 2

    def pair_half(owner, way, sub=0):
        return pair_all.at[owner, pl.ds(way * middle, middle)]

    def flip(owner):
        return owner + 1 - 2 * core

    def w_start(j, ready=lambda sub: None):
        _, _, block = order(j)
        ring_start(block, piece(block, g), functools.partial(quarter, block), 2, ready)

    ring_start(shards, pair_all.at[g], pair_half, 1)
    ring(shards, pair_half, 1, pair_half, lambda: None)
    stage.wait()
    keep_w = pltpu.make_async_copy(
        staged, w_all.at[pl.ds(pl.multiple_of(f * rows, 16), rows)], local_sem.at[0]
    )
    keep_w.start()

    def ready(sub):
        arrive(0, sub)
        if last > 1:

            @pl.when(tied > 0)
            def _():
                arrive(1, sub)

    w_start(0, ready)
    for j in range(last):
        def late():
            @pl.when(j + 1 + tied < last)
            def _():
                for sub in (0, 1):
                    arrive(j + 1 + tied, sub)

            if j + 1 < last:
                w_start(j + 1)

        _, _, block = order(j)
        ring(block, functools.partial(quarter, block), 2, functools.partial(half_piece, block), late)

    ring_finish(
        shards, pair_all.at[g], pair_half, 1, pair_half, pair_all.at[flip(g)],
        lambda owner, way: pair_half(flip(owner), way),
    )
    for side in (0, 1):

        @pl.when(on_line(side))
        def _():
            for sub in (0, 1):
                z_copy(own_part(sub), f, 1, side, sub).wait_send()

    for j in range(last):
        hop, side, block = order(j)
        ring_finish(
            block, piece(block, g), functools.partial(quarter, block), 2, functools.partial(half_piece, block),
            piece(block, flip(g)), lambda owner, way: half_piece(block, flip(owner), way),
        )

        @pl.when(on_line(side))
        def _():
            for sub in (0, 1):
                z_copy(z_piece(block, sub), block, hop + 1, side, sub).wait_send()

    for copy in pair_copies:
        copy.wait_send()
    keep_w.wait()


def gather_all(groups, shards, own_w, own_pair):
    rows, width = own_w.shape
    chips = groups // 2
    any_space = pl.BlockSpec(memory_space=pl.ANY)
    dma = pltpu.SemaphoreType.DMA
    return pl.pallas_call(
        functools.partial(gather_kernel, groups, shards),
        out_shape=(
            jax.ShapeDtypeStruct((shards * rows, width), own_w.dtype),
            jax.ShapeDtypeStruct((groups, shards) + own_pair.shape, own_pair.dtype),
        ),
        in_specs=[any_space, any_space],
        out_specs=(any_space, any_space),
        scratch_shapes=[
            dma((2,)),
            dma((2, 2 * shards)),
            dma((2, 2 * shards)),
            dma((shards,)),
            dma((shards,)),
            dma((shards + 1, chips, 4)),
            dma((shards + 1, chips, 4)),
            dma((shards + 1, chips, 2)),
            dma((shards + 1, chips, 2)),
            pltpu.VMEM(own_w.shape, own_w.dtype),
        ],
        compiler_params=pltpu.CompilerParams(
            collective_id=0,
            has_side_effects=True,
            vmem_limit_bytes=own_w.size * own_w.dtype.itemsize + (8 << 20),
        ),
        name="gather_all",
    )(own_w, own_pair)


def sum_kernel(groups, shards, part, out, in_group, in_shard, mine, total, sem_send, sem_recv):
    g = lax.axis_index("group")
    f = lax.axis_index("fsdp")
    group_to = [(lax.rem(g + k, groups), f) for k in range(1, groups)]
    shard_to = [(g, lax.rem(f + k, shards)) for k in range(1, shards)]
    greet(group_to + shard_to)

    def stage(index, copies):
        for copy in copies:
            copy.start()
        return copies

    first = stage(0, [
        remote(part.at[group_to[k - 1][0]], in_group.at[k], sem_send.at[0, k], sem_recv.at[0, k], group_to[k - 1])
        for k in range(1, groups)
    ])
    total_here = part[g]
    for k, copy in enumerate(first):
        copy.wait_recv()
        total_here = total_here + in_group[k + 1]
    mine[...] = total_here
    second = stage(1, [
        remote(mine.at[shard_to[k - 1][1]], in_shard.at[k], sem_send.at[1, k], sem_recv.at[1, k], shard_to[k - 1])
        for k in range(1, shards)
    ])
    total_here = mine[f]
    for k, copy in enumerate(second):
        copy.wait_recv()
        total_here = total_here + in_shard[k + 1]
    total[g, f] = total_here
    third = stage(2, [
        remote(total.at[g, f], total.at[g, f], sem_send.at[2, k], sem_recv.at[2, k], shard_to[k - 1])
        for k in range(1, shards)
    ])
    for k in range(1, shards):
        source = lax.rem(f + shards - k, shards)
        remote(
            total.at[g, f], total.at[g, source], sem_send.at[2, k], sem_recv.at[2, k], shard_to[k - 1]
        ).wait_recv()
    fourth = stage(3, [
        remote(total.at[g], total.at[g], sem_send.at[3, k], sem_recv.at[3, k], group_to[k - 1])
        for k in range(1, groups)
    ])
    for k in range(1, groups):
        source = lax.rem(g + groups - k, groups)
        remote(
            total.at[g], total.at[source], sem_send.at[3, k], sem_recv.at[3, k], group_to[k - 1]
        ).wait_recv()
    out[...] = total[...]
    for copy in first + second + third + fourth:
        copy.wait_send()


def sum_all(groups, shards, part):
    rows, lanes = part.shape[2:]
    vmem = pl.BlockSpec(memory_space=pltpu.VMEM)
    most = max(groups, shards)
    return pl.pallas_call(
        functools.partial(sum_kernel, groups, shards),
        out_shape=jax.ShapeDtypeStruct(part.shape, part.dtype),
        in_specs=[vmem],
        out_specs=vmem,
        scratch_shapes=[
            pltpu.VMEM((groups, shards, rows, lanes), part.dtype),
            pltpu.VMEM((shards, rows, lanes), part.dtype),
            pltpu.VMEM((shards, rows, lanes), part.dtype),
            pltpu.VMEM(part.shape, part.dtype),
            pltpu.SemaphoreType.DMA((4, most)),
            pltpu.SemaphoreType.DMA((4, most)),
        ],
        compiler_params=pltpu.CompilerParams(collective_id=1, has_side_effects=True),
        name="sum_all",
    )(part)


def on_device(
    groups,
    shards,
    query_embeddings,
    passage_embeddings,
    positives,
    logarithm_scale,
    residual_input,
    attention_head_outputs,
    output_weight,
    adapter_down_weight,
    adapter_up_weight,
    final_norm_weight,
    lengths,
):
    device_count = groups * shards
    own_index = lax.axis_index(("group", "fsdp"))
    q_count, model_width = query_embeddings.shape
    total_queries = q_count * device_count
    logit_scale = jnp.exp(logarithm_scale)
    seq_here, seq_len, _ = residual_input.shape
    heads_width = attention_head_outputs.shape[2]
    rank = adapter_up_weight.shape[0]
    token_rows = attention_head_outputs.reshape(-1, heads_width)

    packed_width = q_count * model_width // 8
    code = jnp.concatenate([positives // code_base, positives % code_base]).astype(jnp.bfloat16)
    code = jnp.broadcast_to(jnp.pad(code, (0, 128 - 2 * q_count))[None, :], (16, 128))
    own_pair = jnp.concatenate(
        [
            jnp.concatenate(
                [query_embeddings.reshape(8, packed_width), passage_embeddings.reshape(8, packed_width)], axis=0
            ),
            code,
        ],
        axis=1,
    )
    full_weight, pairs = gather_all(groups, shards, output_weight, own_pair)
    pairs = pairs.reshape(device_count, 16, packed_width + 128)
    queries = pairs[:, :8, :packed_width].reshape(total_queries, model_width)
    passages = pairs[:, 8:, :packed_width].reshape(total_queries, model_width)
    codes = pairs[:, 0, packed_width : packed_width + 2 * q_count].astype(jnp.int32)
    pos_all = (codes[:, :q_count] * code_base + codes[:, q_count:]).reshape(total_queries)

    logits = logit_scale * lax.dot_general(
        queries, passages, contracted_columns, preferred_element_type=jnp.float32
    )
    hits = jnp.arange(total_queries, dtype=jnp.int32)[None, :] == pos_all[:, None]
    row_max = jnp.max(logits, axis=1)
    log_norm = row_max + jnp.log(jnp.sum(jnp.exp(logits - row_max[:, None]), axis=1))
    pos_logit = jnp.sum(jnp.where(hits, logits, 0.0), axis=1)
    weights = jnp.exp(logits - log_norm[:, None])
    loss = jnp.mean(log_norm - pos_logit)
    scale_grad = jnp.mean(jnp.sum(weights * logits, axis=1) - pos_logit)
    weight_half = weights.astype(jnp.bfloat16)
    hot_half = hits.astype(jnp.bfloat16)
    first_own = own_index * q_count
    own_rows = jnp.concatenate(
        [
            lax.dynamic_slice_in_dim(weight_half, first_own, q_count, 0),
            lax.dynamic_slice_in_dim(hot_half, first_own, q_count, 0),
        ],
        axis=0,
    )
    own_columns = jnp.concatenate(
        [
            lax.dynamic_slice_in_dim(weight_half, first_own, q_count, 1),
            lax.dynamic_slice_in_dim(hot_half, first_own, q_count, 1),
        ],
        axis=1,
    )
    by_query = jnp.dot(own_rows, passages, preferred_element_type=jnp.float32)
    query_grad = logit_scale * (by_query[:q_count] - by_query[q_count:])
    by_passage = lax.dot_general(own_columns, queries, contract_rows, preferred_element_type=jnp.float32)
    passage_grad = logit_scale * (by_passage[:q_count] - by_passage[q_count:])

    reduced_activation = jnp.dot(
        token_rows, adapter_down_weight, preferred_element_type=jnp.float32
    ).astype(jnp.bfloat16)
    hidden_state = (
        residual_input.reshape(-1, model_width).astype(jnp.float32)
        + jnp.dot(token_rows, full_weight, preferred_element_type=jnp.float32)
        + adapter_scale
        * jnp.dot(reduced_activation, adapter_up_weight, preferred_element_type=jnp.float32)
    )
    row_grads = query_grad[:seq_here]
    position = jnp.arange(seq_len, dtype=jnp.int32)
    weight = (
        grad_scale
        * (position[None, :] < lengths[:, None]).astype(jnp.float32)
        / lengths[:, None].astype(jnp.float32)
    )
    gained = (
        weight[:, :, None] * row_grads[:, None, :] * final_norm_weight[None, None, :]
    ).reshape(-1, model_width)
    inv_rms = lax.rsqrt(jnp.mean(hidden_state * hidden_state, axis=1) + epsilon)
    hidden_grad = (
        inv_rms[:, None] * gained
        - hidden_state
        * (inv_rms * inv_rms * inv_rms * jnp.mean(gained * hidden_state, axis=1))[:, None]
    )
    gradient_portion = hidden_grad.astype(jnp.bfloat16)
    reduced_gradient = (
        adapter_scale
        * lax.dot_general(
            gradient_portion,
            adapter_up_weight,
            contracted_columns,
            preferred_element_type=jnp.float32,
        )
    ).astype(jnp.bfloat16)
    down_part = lax.dot_general(
        reduced_gradient, token_rows, contract_rows, preferred_element_type=jnp.float32
    )
    up_part = adapter_scale * lax.dot_general(
        reduced_activation, gradient_portion, contract_rows, preferred_element_type=jnp.float32
    )
    both = jnp.concatenate([down_part.reshape(-1, 128), up_part.reshape(-1, 128)], axis=0)
    summed = sum_all(groups, shards, both.reshape(groups, shards, -1, 128)).reshape(-1, 128)
    summed = summed / (seq_here * device_count)
    down_rows = rank * heads_width // 128
    down_total = summed[:down_rows].reshape(rank, heads_width).T
    up_total = summed[down_rows:].reshape(rank, model_width)
    head_gradient = (
        lax.dot_general(
            gradient_portion, full_weight, contracted_columns, preferred_element_type=jnp.float32
        )
        + lax.dot_general(
            reduced_gradient,
            adapter_down_weight,
            contracted_columns,
            preferred_element_type=jnp.float32,
        )
    ).astype(jnp.bfloat16)
    return (
        loss,
        scale_grad,
        query_grad,
        passage_grad,
        head_gradient.reshape(seq_here, seq_len, heads_width),
        gradient_portion.reshape(seq_here, seq_len, model_width),
        down_total,
        up_total,
    )


def solution(mesh):
    both = ("group", "fsdp")
    placed = (
        P(both, None),
        P(both, None),
        P(both),
        P(),
        P(both, None, None),
        P(both, None, None),
        P("fsdp", None),
        P(),
        P(),
        P(),
        P(both),
    )
    return jax.shard_map(
        functools.partial(on_device, mesh.shape["group"], mesh.shape["fsdp"]),
        mesh=mesh,
        in_specs=placed,
        out_specs=(
            P(),
            P(),
            P(both, None),
            P(both, None),
            P(both, None, None),
            P(both, None, None),
            P(),
            P(),
        ),
        check_vma=False,
    )
```
